32 devices in a mesh: inner: 4 (over x, core), outer: 8 (over z, y).
Axes of the slice: x: 2, y: 2, z: 4, core: 2. Of those that a mesh axis runs over, the one named last changes fastest.
Arguments:
- slices: float32 [8, 4, 256, 256], P('outer', 'inner'), may hold values from -1 to 1, as said below
- weight: float32 [8, 4, 256, 256], P('outer', 'inner'), may hold values from -6 to 6
Outputs:
- gradient: float32 [8, 4, 256, 256], P('outer', 'inner')
The draws below stay inside these ranges and needn't reach their ends.
Inputs may be any that keep to these rules, and one draw needn't show every extreme that they name: `slices`: every slice is an orthogonal matrix up to float32 rounding (only up to rounding: products of its transpose with it differ from the identity by rounding errors).
All inputs are finite; a program needn't handle non-finite values.
Results may differ from the reference program's by a relative error of at most 0.0003.
Values sent between devices are 32-bit elements; how exact they have to be, the bound alone decides.
No kernel may reach another device: no remote copies, remote signals or barrier semaphores. Data moves between devices by JAX's collectives and lax.ppermute only.
A program may use at most 64 MiB of HBM per device.

```python
import jax
import jax.numpy as jnp
from jax import lax

DIM = 256
STEPS_IN = 4
STEPS_OUT = 8


def draw_slices(key, part):
    raw = jax.random.normal(key, (STEPS_OUT * STEPS_IN, DIM, DIM), jnp.float32)
    factor = 0.5
    eye = jnp.eye(DIM, dtype=jnp.float32)

    def cayley(block):
        skew = (block - block.T) * (factor / DIM ** 0.5)
        return jnp.linalg.solve(eye - skew, eye + skew)
    mats = lax.map(cayley, raw)
    return mats.reshape(STEPS_OUT, STEPS_IN, DIM, DIM)


def levels(stream_key, extent, split, low, largest):
    level = 1.0
    for dim, shards_of in split:
        steps = jax.random.uniform(jax.random.fold_in(jax.random.fold_in(stream_key, 6), dim), (shards_of,), jnp.float32, low / len(split), largest / len(split))
        level = level * jnp.repeat(jnp.exp(steps), extent[dim] // shards_of).reshape((-1,) + (1,) * (len(extent) - 1 - dim))
    return level


def noise(stream_key, extent, spread, bound, pieces=(), kind=jnp.bfloat16):
    factor_of = levels(stream_key, extent, pieces, -0.22, 0.18) if pieces else 1.0
    drawn = jax.random.normal(stream_key, extent, jnp.float32) * spread * factor_of
    return jnp.minimum(jnp.maximum(drawn, -bound), bound).astype(kind)


def setup_inputs(seed: int = 0) -> dict:
    key_of = jax.random.split(jax.random.key(seed), 3)
    return {
        "slices": draw_slices(jax.random.fold_in(key_of[2], 71), 0),
        "weight": noise(key_of[1], (STEPS_OUT, STEPS_IN, DIM, DIM), 1.0, 6.0, ((0, 8), (1, 4)), jnp.float32),
    }


def matmul(left, right):
    return jnp.dot(left.astype(jnp.float32), right.astype(jnp.float32), precision=lax.Precision.HIGHEST, preferred_element_type=jnp.float32)

def reference(slices, weight):
    flat = slices.reshape(-1, DIM, DIM)
    flat_weight = weight.reshape(-1, DIM, DIM)

    def advance(carry, unit):
        nxt = matmul(unit, carry)
        return (nxt, nxt)

    def retreat(carry, unit):
        nxt = matmul(carry, unit)
        return (nxt, carry)
    start = jnp.eye(DIM, dtype=jnp.float32)
    last, forward = lax.scan(advance, start, flat)
    first, back = lax.scan(retreat, start, flat, reverse=True)

    def project(triple):
        return matmul(matmul(triple[0].T, triple[1]), triple[2])
    gradient = lax.map(project, (back, flat_weight, forward))
    return gradient.reshape(slices.shape)
```

```python
import jax
import jax.numpy as jnp
from jax import lax
from jax.sharding import PartitionSpec as P


def dot(left, right):
    return jnp.dot(left, right, precision=lax.Precision.HIGHEST, preferred_element_type=jnp.float32)


def dot_nt(left, right):
    dims = (((1,), (1,)), ((), ()))
    return lax.dot_general(left, right, dims, precision=lax.Precision.HIGHEST, preferred_element_type=jnp.float32)


def dot_tn(left, right):
    dims = (((0,), (0,)), ((), ()))
    return lax.dot_general(left, right, dims, precision=lax.Precision.HIGHEST, preferred_element_type=jnp.float32)


def ordered(first, a, b):
    return jnp.where(first, a, b), jnp.where(first, b, a)


class Group:
    def __init__(self, n_in, n_out):
        self.n = n_in * n_out
        self.place = [(k % n_in) * n_out + k // n_in for k in range(self.n)]
        self.index = lax.axis_index("outer") * n_in + lax.axis_index("inner")

    def bit(self, b):
        return (self.index >> b) & 1 == 1

    def send(self, value, even, odd=None):
        pairs = []
        for k in range(self.n):
            mask = odd if k & 1 else even
            if mask is not None:
                pairs.append((self.place[k], self.place[k ^ mask]))
        return lax.ppermute(value, ("inner", "outer"), pairs)

    def swap(self, value, mask):
        return self.send(value, mask, mask)


def join(group, b, by, before, after):
    flag = group.bit(b)
    new = dot(jnp.where(flag, before, by), jnp.where(flag, by, after))
    return jnp.where(flag, new, before), jnp.where(flag, after, new)


def pairwise(group, bits, total, before, after):
    for b in bits:
        by = group.swap(total, 1 << b)
        before, after = join(group, b, by, before, after)
        total = dot(*ordered(group.bit(b), total, by))
    return before, after


def body(n_in, n_out, slices, weight):
    group = Group(n_in, n_out)
    mine, w = slices[0, 0], weight[0, 0]
    order = mine.shape[0]
    part = order // 2
    eye = jnp.eye(order, dtype=jnp.float32)
    bits = group.n.bit_length() - 1
    if bits < 5:
        before, after = pairwise(group, range(bits), mine, mine, eye)
        return dot(dot_tn(after, w), before)[None, None]
    second = group.bit(0)

    def whole(piece):
        other = group.swap(piece, 1)
        return jnp.concatenate([jnp.where(second, other, piece), jnp.where(second, piece, other)], axis=0)

    def pair_of_pairs(product):
        other = group.swap(product, 1)
        return jnp.where(second, other, product), jnp.where(second, product, other)

    other = group.swap(mine, 1)
    chip = dot(*ordered(second, mine, other))
    wide = group.send(chip, 24, 6)
    close = group.send(chip, 2, 4)
    product = dot(*ordered(group.bit(1), jnp.where(second, close, chip), jnp.where(second, wide, close)))
    beside = group.send(wide, 2)
    near, far = pair_of_pairs(product)
    left, right = ordered(group.bit(2), near, far)
    four_piece = dot(lax.dynamic_slice_in_dim(left, (group.index & 1) * part, part, 0), right)
    one_piece, two_piece = group.swap(four_piece, 8), group.swap(four_piece, 16)
    flag = group.bit(1)
    left = jnp.where(second, near, jnp.where(flag, mine, close))
    right = jnp.where(second, jnp.where(flag, eye, chip.T), jnp.where(flag, close, other))
    new = dot(left, right)
    before = jnp.where(flag, new, jnp.where(second, chip, mine))
    after = jnp.where(flag, jnp.where(second, eye, other), new)
    before, after = join(group, 2, far, before, after)
    product = dot(*ordered(group.bit(1), wide, beside))
    across = group.send(product, 5)
    three = dot(*ordered(group.bit(2), *pair_of_pairs(jnp.where(second, across, product))))
    one, two = whole(one_piece), whole(two_piece)
    if bits > 5:
        four = dot(left, right)
        eight = dot(*ordered(group.bit(3), four, one))
        others = dot(*ordered(group.bit(3), two, three))
        before, after = join(group, 3, one, before, after)
        before, after = join(group, 4, others, before, after)
        total = dot(*ordered(group.bit(4), eight, others))
        before, after = pairwise(group, range(5, bits), total, before, after)
        return dot(dot_tn(after, w), before)[None, None]
    after_t = after.T
    wp = dot(w, before)

    def start0():
        return dot_nt(after_t, one), dot_tn(three, wp)

    def start1():
        return dot_nt(after_t, three), dot(wp, one)

    def start2():
        return dot(dot(dot_nt(after_t, one), wp), three), three

    def start3():
        return dot(dot(after_t, wp), one), three

    def end0():
        return dot(dot_nt(a, two), b)

    def end2():
        return dot(a, two)

    def end3():
        return dot(dot(a, two), b)

    which = (group.index >> 3) & 3
    a, b = lax.switch(which, [start0, start1, start2, start3])
    result = lax.switch(which, [end0, end0, end2, end3])
    return result[None, None]


def solution(mesh):
    spec = P("outer", "inner", None, None)
    n_in, n_out = mesh.shape["inner"], mesh.shape["outer"]

    def run(slices, weight):
        return body(n_in, n_out, slices, weight)

    return jax.shard_map(run, mesh=mesh, in_specs=(spec, spec), out_specs=spec, check_vma=False)
```

```python
import functools

import jax
import jax.numpy as jnp
from jax import lax
from jax.experimental import pallas as pl
from jax.experimental.pallas import tpu as pltpu
from jax.sharding import PartitionSpec as P


FAR = 200


def halves(value):
    high = value.astype(jnp.bfloat16)
    return high, (value - high.astype(jnp.float32)).astype(jnp.bfloat16)


def product(left, right, dims):
    def one_pass(a, b):
        return lax.dot_general(a, b, (dims, ((), ())), preferred_element_type=jnp.float32)

    (left_high, left_low), (right_high, right_low) = halves(left), halves(right)
    cross = one_pass(left_high, right_low) + one_pass(left_low, right_high)
    return one_pass(left_high, right_high) + cross


def mul(left, right):
    return product(left, right, ((1,), (0,)))


def mul_nt(left, right):
    return product(left, right, ((1,), (1,)))


def mul_tn(left, right):
    return product(left.T, right, ((1,), (0,)))


def dot(left, right):
    return jnp.dot(left, right, precision=lax.Precision.HIGHEST, preferred_element_type=jnp.float32)


def ordered(first, a, b):
    return jnp.where(first, a, b), jnp.where(first, b, a)


class Group:
    def __init__(self, n_in, n_out):
        self.n_in, self.n = n_in, n_in * n_out
        self.place = [(k % n_in) * n_out + k // n_in for k in range(self.n)]

    def bit(self, b):
        return ((lax.axis_index("outer") * self.n_in + lax.axis_index("inner")) >> b) & 1 == 1

    def send(self, value, even, odd):
        pairs = [(self.place[k], self.place[k ^ (odd if k & 1 else even)]) for k in range(self.n)]
        return lax.ppermute(value, ("inner", "outer"), pairs)

    def swap(self, value, mask):
        return self.send(value, mask, mask)


def run(body, group, shapes, *operands, scratch=(), weight=1):
    order = operands[0].shape[-1]
    whole = pl.BlockSpec(memory_space=pltpu.VMEM)
    return pl.pallas_call(
        functools.partial(body, group),
        out_shape=[jax.ShapeDtypeStruct(shape, jnp.float32) for shape in shapes],
        in_specs=[whole] * len(operands),
        out_specs=[whole] * len(shapes),
        scratch_shapes=[pltpu.VMEM(shape, jnp.float32) for shape in scratch],
        compiler_params=pltpu.CompilerParams(vmem_limit_bytes=16 * 2**20),
        cost_estimate=pl.CostEstimate(flops=6 * weight * order**3, bytes_accessed=0, transcendentals=0),
    )(*operands)


def when(flag, then, other):
    pl.when(flag)(then)
    pl.when(jnp.logical_not(flag))(other)


def in_order(flag, out, a, b):
    def first():
        out[...] = mul(a[...], b[...])

    def last():
        out[...] = mul(b[...], a[...])

    when(flag, first, last)


def chip_kernel(group, mine, other, chip):
    in_order(group.bit(0), chip, mine, other)


def pair_kernel(group, chip, close, wide, pair, sent):
    def first():
        in_order(group.bit(1), pair, chip, close)
        sent[...] = wide[...]

    def second():
        in_order(group.bit(1), pair, close, wide)
        sent[...] = pair[...]

    when(group.bit(0), second, first)


def four_kernel(group, pair, given, to_d, to_y, to_x):
    def first():
        in_order(group.bit(2), to_d, pair, given)
        to_y[...] = to_d[...]
        to_x[...] = pair[...]

    def second():
        for out in (to_d, to_y, to_x):
            out[...] = given[...]

    when(group.bit(0), second, first)


def own_kernel(group, mine, other, chip, close, pair, given, by_x, w, after, wp, before, far):
    @pl.when(jnp.logical_not(group.bit(0)))
    def _():
        far[...] = given[...]

        def late():
            before[...] = mul(mine[...], close[...])
            after[...] = other[...]

        def early():
            before[...] = mine[...]
            after[...] = mul(close[...], other[...])

        when(group.bit(1), late, early)

    @pl.when(group.bit(0))
    def _():
        far[...] = pair[...]

        def late():
            before[...] = by_x[...]
            row = lax.broadcasted_iota(jnp.int32, after.shape, 0)
            column = lax.broadcasted_iota(jnp.int32, after.shape, 1)
            after[...] = jnp.where(row == column, 1.0, 0.0)

        def early():
            before[...] = chip[...]
            after[...] = mul_nt(by_x[...], chip[...])

        when(group.bit(1), late, early)

    def late():
        before[...] = mul(before[...], far[...])

    def early():
        after[...] = mul(far[...], after[...])

    when(group.bit(2), late, early)
    wp[...] = mul(w[...], before[...])


def near_kernel(group, wide, by_x, by_y, both):
    def first():
        in_order(group.bit(1), both.at[0], wide, by_x)

    def second():
        both[0] = wide[...]

    when(group.bit(0), second, first)
    both[1] = by_y[...]


def far_kernel(group, by_y, by_d, far):
    def first():
        far[...] = by_d[...]

    def second():
        in_order(group.bit(1), far, by_y, by_d)

    when(group.bit(0), second, first)


def held_kernel(group, both, far, held):
    def first():
        held[...] = far[...]

    def second():
        in_order(group.bit(2), held, both.at[0], far)

    when(group.bit(0), second, first)


def sides_kernel(group, after, wp, by_y, both, held, a, b, one):
    second, odd, upper = group.bit(0), group.bit(3), group.bit(4)
    one[...] = jnp.where(second, both[1], by_y[...])

    @pl.when(jnp.logical_not(odd))
    def _():
        a[...] = mul(one[...], after[...]).T

    @pl.when(jnp.logical_not(upper))
    def _():
        def later():
            a[...] = after[...].T
            b[...] = mul(wp[...], one[...])

        def first():
            b[...] = wp[...]

        when(odd, later, first)

        def left():
            a[...] = mul_nt(a[...], held[...])

        def right():
            b[...] = mul_tn(held[...], b[...])

        when(odd == second, left, right)

    @pl.when(upper)
    def _():
        def later():
            a[...] = mul(mul_tn(after[...], wp[...]), one[...])

        def first():
            a[...] = mul(a[...], wp[...])

        when(odd, later, first)

        def left():
            a[...] = mul(a[...], held[...])

        def right():
            b[...] = held[...]

        when(odd != second, left, right)


def result_kernel(group, a, come, b, result):
    upper, whole = group.bit(4), group.bit(4) & (group.bit(3) != group.bit(0))

    @pl.when(jnp.logical_not(upper))
    def _():
        result[...] = mul(mul_nt(a[...], come[...]), b[...])

    @pl.when(whole)
    def _():
        result[...] = mul(a[...], come[...])

    @pl.when(upper & jnp.logical_not(whole))
    def _():
        result[...] = mul(mul(a[...], come[...]), b[...])


def join(group, b, by, wp, after):
    flag = group.bit(b)
    new = dot(jnp.where(flag, wp, by), jnp.where(flag, by, after))
    return jnp.where(flag, new, wp), jnp.where(flag, after, new)


def pairwise(group, bits, total, wp, after):
    for b in bits:
        by = group.swap(total, 1 << b)
        wp, after = join(group, b, by, wp, after)
        total = dot(*ordered(group.bit(b), total, by))
    return dot(after.T, wp)


def body(n_in, n_out, slices, weight):
    group = Group(n_in, n_out)
    mine, w = slices[0, 0], weight[0, 0]
    square = mine.shape
    bits = group.n.bit_length() - 1
    if bits < 5:
        return pairwise(group, range(bits), mine, dot(w, mine), jnp.eye(square[0], dtype=jnp.float32))[None, None]
    other = group.swap(mine, 1)
    mine = lax.optimization_barrier(jnp.where(lax.axis_index("inner") < n_in, mine, 0.0))
    (chip,) = run(chip_kernel, group, [square], mine, other)
    wide = group.send(chip, 24, 6)
    close = group.send(chip, 2, 4)
    pair, sent = run(pair_kernel, group, [square] * 2, chip, close, wide)
    given = group.swap(sent, 1)
    to_d, to_y, to_x = run(four_kernel, group, [square] * 3, pair, given)
    by_d, by_x, by_y = group.send(to_d, 16, 6), group.send(to_x, 1, 3), group.send(to_y, 8, 4)
    after, wp = run(
        own_kernel, group, [square] * 2, mine, other, chip, close, pair, given, by_x, w, scratch=[square] * 2, weight=3
    )
    by_x, by_y, after, wp = lax.optimization_barrier((by_x, by_y, after, wp))
    (both,) = run(near_kernel, group, [(2, *square)], wide, by_x, by_y)
    both = group.swap(both, 1)
    (far,) = run(far_kernel, group, [square], by_y, by_d, weight=FAR)
    (held,) = run(held_kernel, group, [square], both, far)
    come = group.swap(held, 1)
    if bits > 5:
        second = group.bit(0)
        one = jnp.where(second, both[1], by_y)
        two, three = jnp.where(second, come, held), jnp.where(second, held, come)
        four = jnp.where(second, group.swap(to_d, 1), to_d)
        eight = dot(*ordered(group.bit(3), four, one))
        others = dot(*ordered(group.bit(3), two, three))
        wp, after = join(group, 3, one, wp, after)
        wp, after = join(group, 4, others, wp, after)
        total = dot(*ordered(group.bit(4), eight, others))
        return pairwise(group, range(5, bits), total, wp, after)[None, None]
    a, b = run(sides_kernel, group, [square] * 2, after, wp, by_y, both, held, scratch=[square], weight=3)
    (result,) = run(result_kernel, group, [square], a, come, b, weight=2)
    return result[None, None]


def solution(mesh):
    spec = P("outer", "inner", None, None)
    n_in, n_out = mesh.shape["inner"], mesh.shape["outer"]

    def gradient(slices, weight):
        return body(n_in, n_out, slices, weight)

    return jax.shard_map(gradient, mesh=mesh, in_specs=(spec, spec), out_specs=spec, check_vma=False)
```

```python
import functools

import jax
import jax.numpy as jnp
from jax import lax
from jax.experimental import pallas as pl
from jax.experimental.pallas import tpu as pltpu
from jax.sharding import PartitionSpec as P


def halves(value):
    high = value.astype(jnp.bfloat16)
    return high, (value - high.astype(jnp.float32)).astype(jnp.bfloat16)


def product(left, right, dims):
    def one_pass(a, b):
        return lax.dot_general(a, b, (dims, ((), ())), preferred_element_type=jnp.float32)

    (left_high, left_low), (right_high, right_low) = halves(left), halves(right)
    cross = one_pass(left_high, right_low) + one_pass(left_low, right_high)
    return one_pass(left_high, right_high) + cross


def mul(left, right):
    return product(left, right, ((1,), (0,)))


def mul_nt(left, right):
    return product(left, right, ((1,), (1,)))


def mul_tn(left, right):
    return product(left.T, right, ((1,), (0,)))


def dot(left, right):
    return jnp.dot(left, right, precision=lax.Precision.HIGHEST, preferred_element_type=jnp.float32)


def ordered(first, a, b):
    return jnp.where(first, a, b), jnp.where(first, b, a)


class Group:
    def __init__(self, n_in, n_out):
        self.n_in, self.n = n_in, n_in * n_out
        self.place = [(k % n_in) * n_out + k // n_in for k in range(self.n)]

    def bit(self, b):
        return ((lax.axis_index("outer") * self.n_in + lax.axis_index("inner")) >> b) & 1 == 1

    def send(self, value, even, odd):
        pairs = [(self.place[k], self.place[k ^ (odd if k & 1 else even)]) for k in range(self.n)]
        return lax.ppermute(value, ("inner", "outer"), pairs)

    def swap(self, value, mask):
        return self.send(value, mask, mask)


def run(body, group, shapes, *operands, scratch=(), weight=1):
    order = operands[0].shape[-1]
    whole = pl.BlockSpec(memory_space=pltpu.VMEM)
    return pl.pallas_call(
        functools.partial(body, group),
        out_shape=[jax.ShapeDtypeStruct(shape, jnp.float32) for shape in shapes],
        in_specs=[whole] * len(operands),
        out_specs=[whole] * len(shapes),
        scratch_shapes=[pltpu.VMEM(shape, jnp.float32) for shape in scratch],
        compiler_params=pltpu.CompilerParams(vmem_limit_bytes=16 * 2**20),
        cost_estimate=pl.CostEstimate(flops=6 * weight * order**3, bytes_accessed=0, transcendentals=0),
    )(*operands)


def when(flag, then, other):
    pl.when(flag)(then)
    pl.when(jnp.logical_not(flag))(other)


def in_order(flag, out, a, b):
    def first():
        out[...] = mul(a[...], b[...])

    def last():
        out[...] = mul(b[...], a[...])

    when(flag, first, last)


def chip_kernel(group, mine, other, chip):
    in_order(group.bit(0), chip, mine, other)


def pair_kernel(group, chip, close, wide, pair, sent):
    def first():
        in_order(group.bit(1), pair, chip, close)
        sent[...] = wide[...]

    def second():
        in_order(group.bit(1), pair, close, wide)
        sent[...] = pair[...]

    when(group.bit(0), second, first)


def four_kernel(group, pair, given, four, to_y, to_x):
    def first():
        in_order(group.bit(2), four, pair, given)
        to_x[...] = pair[...]

    def second():
        four[...] = given[...]
        to_x[...] = given[...]

    when(group.bit(0), second, first)
    to_y[...] = four[...]


def keep_kernel(group, value, kept):
    kept[...] = value[...]


def own_kernel(group, mine, other, chip, close, pair, given, by_x, w, after, wp, before, far):
    @pl.when(jnp.logical_not(group.bit(0)))
    def _():
        far[...] = given[...]

        def late():
            before[...] = mul(mine[...], close[...])
            after[...] = other[...]

        def early():
            before[...] = mine[...]
            after[...] = mul(close[...], other[...])

        when(group.bit(1), late, early)

    @pl.when(group.bit(0))
    def _():
        far[...] = pair[...]

        def late():
            before[...] = by_x[...]
            row = lax.broadcasted_iota(jnp.int32, after.shape, 0)
            column = lax.broadcasted_iota(jnp.int32, after.shape, 1)
            after[...] = jnp.where(row == column, 1.0, 0.0)

        def early():
            before[...] = chip[...]
            after[...] = mul_nt(by_x[...], chip[...])

        when(group.bit(1), late, early)

    def late():
        before[...] = mul(before[...], far[...])

    def early():
        after[...] = mul(far[...], after[...])

    when(group.bit(2), late, early)
    wp[...] = mul(w[...], before[...])


def near_kernel(group, wide, by_x, near):
    def first():
        in_order(group.bit(1), near, wide, by_x)

    def second():
        near[...] = wide[...]

    when(group.bit(0), second, first)


def sides_kernel(group, after, wp, near, their_near, by_d, by_y, a, b, three, held):
    second, near_left, odd, upper = group.bit(0), group.bit(2), group.bit(3), group.bit(4)

    def on_first():
        two, one = by_d, by_y

        @pl.when(jnp.logical_not(odd))
        def _():
            held[...] = mul(one[...], after[...])

        def early():
            def odd_four():
                a[...] = mul(mul(mul_tn(after[...], wp[...]), one[...]), two[...])

            def even_four():
                a[...] = mul_tn(held[...], wp[...])
                b[...] = two[...]

            when(odd, odd_four, even_four)

            def left():
                a[...] = mul(a[...], near[...])

            def right():
                def odd_four():
                    b[...] = near[...]

                def even_four():
                    b[...] = mul(near[...], two[...])

                when(odd, odd_four, even_four)

            when(near_left, left, right)

        def late():
            def odd_four():
                a[...] = after[...].T
                b[...] = mul_tn(two[...], mul(wp[...], one[...]))

            def even_four():
                a[...] = mul(two[...], held[...]).T
                b[...] = wp[...]

            when(odd, odd_four, even_four)

            def right():
                b[...] = mul_tn(near[...], b[...])

            def left():
                a[...] = mul_nt(a[...], near[...])

            when(near_left, right, left)

        when(upper, early, late)

    def on_second():
        in_order(group.bit(1), held, by_y, by_d)
        in_order(near_left, three, their_near, held)

        def early():
            def odd_four():
                a[...] = mul_tn(after[...], wp[...])
                b[...] = three[...]

            def even_four():
                a[...] = after[...].T
                b[...] = mul(wp[...], three[...])

            when(odd, odd_four, even_four)

        def late():
            def odd_four():
                a[...] = mul(three[...], after[...]).T
                b[...] = wp[...]

            def even_four():
                a[...] = after[...].T
                b[...] = mul_tn(three[...], wp[...])

            when(odd, odd_four, even_four)

        when(upper, early, late)

    when(second, on_second, on_first)


def closer_kernel(group, a, b, come, new_a, new_b):
    second, x_bit, near_left, odd, upper = (group.bit(k) for k in range(5))
    new_a[...] = a[...]
    new_b[...] = b[...]

    def on_first():
        def early():
            def right():
                def alone():
                    new_b[...] = come[...]

                def beside():
                    new_b[...] = mul(come[...], b[...])

                when(odd & near_left, alone, beside)

            def left():
                new_a[...] = mul(a[...], come[...])

            when(x_bit, right, left)

        def late():
            def left():
                new_a[...] = mul_nt(a[...], come[...])

            def right():
                new_b[...] = mul_tn(come[...], b[...])

            when(x_bit, left, right)

        when(upper, early, late)

    def on_second():
        def early():
            in_order(odd, new_b, come, b)

        def late():
            def odd_four():
                new_a[...] = mul(mul_nt(a[...], come[...]), b[...])

            def even_four():
                new_b[...] = mul_tn(come[...], b[...])

            when(odd, odd_four, even_four)

        when(upper, early, late)

    when(second, on_second, on_first)


def result_kernel(group, a, b, come, result, mid):
    second, x_bit, near_left, odd, upper = (group.bit(k) for k in range(5))
    plain = jnp.where(second, odd, upper)
    alone = odd & jnp.where(second, jnp.logical_not(upper), upper & near_left & jnp.logical_not(x_bit))

    def as_is():
        mid[...] = mul(a[...], come[...])

    def transposed():
        mid[...] = mul_nt(a[...], come[...])

    when(plain, as_is, transposed)

    def last():
        result[...] = mid[...]

    def one_more():
        result[...] = mul(mid[...], b[...])

    when(alone, last, one_more)


def join(group, b, by, wp, after):
    flag = group.bit(b)
    new = dot(jnp.where(flag, wp, by), jnp.where(flag, by, after))
    return jnp.where(flag, new, wp), jnp.where(flag, after, new)


def pairwise(group, bits, total, wp, after):
    for b in bits:
        by = group.swap(total, 1 << b)
        wp, after = join(group, b, by, wp, after)
        total = dot(*ordered(group.bit(b), total, by))
    return dot(after.T, wp)


def body(n_in, n_out, slices, weight):
    group = Group(n_in, n_out)
    mine, w = slices[0, 0], weight[0, 0]
    square = mine.shape
    bits = group.n.bit_length() - 1
    if bits < 5:
        return pairwise(group, range(bits), mine, dot(w, mine), jnp.eye(square[0], dtype=jnp.float32))[None, None]
    other = group.swap(mine, 1)
    mine = lax.optimization_barrier(jnp.where(lax.axis_index("inner") < n_in, mine, 0.0))
    (chip,) = run(chip_kernel, group, [square], mine, other)
    wide = group.send(chip, 24, 6)
    close = group.send(chip, 2, 4)
    pair, sent = run(pair_kernel, group, [square] * 2, chip, close, wide)
    given = group.swap(sent, 1)
    four, to_y, to_x = run(four_kernel, group, [square] * 3, pair, given)
    by_x, by_d, by_y = group.send(to_x, 1, 3), group.send(four, 16, 6), group.send(to_y, 8, 4)
    after, wp = run(
        own_kernel, group, [square] * 2, mine, other, chip, close, pair, given, by_x, w, scratch=[square] * 2, weight=3
    )
    by_x, after, wp = lax.optimization_barrier((by_x, after, wp))
    (near,) = run(near_kernel, group, [square], wide, by_x)
    their_near = group.swap(near, 1)
    their_d = group.swap(by_d, 1)
    by_y, by_d = lax.optimization_barrier((by_y, *run(keep_kernel, group, [square], by_d)))
    their_y = group.swap(by_y, 1)
    if bits > 5:
        second = group.bit(0)
        one, two = jnp.where(second, their_y, by_y), jnp.where(second, their_d, by_d)
        far = dot(*ordered(group.bit(1), jnp.where(second, by_y, their_y), jnp.where(second, by_d, their_d)))
        three = dot(*ordered(group.bit(2), jnp.where(second, their_near, near), far))
        four = jnp.where(second, group.swap(four, 1), four)
        eight = dot(*ordered(group.bit(3), four, one))
        others = dot(*ordered(group.bit(3), two, three))
        wp, after = join(group, 3, one, wp, after)
        wp, after = join(group, 4, others, wp, after)
        total = dot(*ordered(group.bit(4), eight, others))
        return pairwise(group, range(5, bits), total, wp, after)[None, None]
    a, b = run(
        sides_kernel, group, [square] * 2, after, wp, near, their_near, by_d, by_y, scratch=[square] * 2, weight=4
    )
    a, b = run(closer_kernel, group, [square] * 2, a, b, their_d)
    (result,) = run(result_kernel, group, [square], a, b, their_y, scratch=[square], weight=2)
    return result[None, None]


def solution(mesh):
    spec = P("outer", "inner", None, None)
    n_in, n_out = mesh.shape["inner"], mesh.shape["outer"]

    def gradient(slices, weight):
        return body(n_in, n_out, slices, weight)

    return jax.shard_map(gradient, mesh=mesh, in_specs=(spec, spec), out_specs=spec, check_vma=False)
```

```python
import functools

import jax
import jax.numpy as jnp
from jax import lax
from jax.experimental import pallas as pl
from jax.experimental.pallas import tpu as pltpu
from jax.sharding import PartitionSpec as P


def halves(value):
    high = value.astype(jnp.bfloat16)
    return high, (value - high.astype(jnp.float32)).astype(jnp.bfloat16)


def product(left, right, dims):
    def one_pass(a, b):
        return lax.dot_general(a, b, (dims, ((), ())), preferred_element_type=jnp.float32)

    (left_high, left_low), (right_high, right_low) = halves(left), halves(right)
    cross = one_pass(left_high, right_low) + one_pass(left_low, right_high)
    return one_pass(left_high, right_high) + cross


def mul(left, right):
    return product(left, right, ((1,), (0,)))


def mul_nt(left, right):
    return product(left, right, ((1,), (1,)))


def mul_tn(left, right):
    return product(left.T, right, ((1,), (0,)))


def dot(left, right):
    return jnp.dot(left, right, precision=lax.Precision.HIGHEST, preferred_element_type=jnp.float32)


def ordered(first, a, b):
    return jnp.where(first, a, b), jnp.where(first, b, a)


class Group:
    def __init__(self, n_in, n_out):
        self.n_in, self.n = n_in, n_in * n_out
        self.place = [(k % n_in) * n_out + k // n_in for k in range(self.n)]

    def bit(self, b):
        return ((lax.axis_index("outer") * self.n_in + lax.axis_index("inner")) >> b) & 1 == 1

    def send(self, value, even, odd):
        pairs = [(self.place[k], self.place[k ^ (odd if k & 1 else even)]) for k in range(self.n)]
        return lax.ppermute(value, ("inner", "outer"), pairs)

    def swap(self, value, mask):
        return self.send(value, mask, mask)


def run(body, group, shapes, *operands, scratch=(), weight=1):
    order = operands[0].shape[-1]
    whole = pl.BlockSpec(memory_space=pltpu.VMEM)
    return pl.pallas_call(
        functools.partial(body, group),
        out_shape=[jax.ShapeDtypeStruct(shape, jnp.float32) for shape in shapes],
        in_specs=[whole] * len(operands),
        out_specs=[whole] * len(shapes),
        scratch_shapes=[pltpu.VMEM(shape, jnp.float32) for shape in scratch],
        compiler_params=pltpu.CompilerParams(vmem_limit_bytes=16 * 2**20),
        cost_estimate=pl.CostEstimate(flops=6 * weight * order**3, bytes_accessed=0, transcendentals=0),
    )(*operands)


def when(flag, then, other):
    pl.when(flag)(then)
    pl.when(jnp.logical_not(flag))(other)


def in_order(flag, out, a, b):
    def first():
        out[...] = mul(a[...], b[...])

    def last():
        out[...] = mul(b[...], a[...])

    when(flag, first, last)


def chip_kernel(group, mine, other, chip):
    in_order(group.bit(0), chip, mine, other)


def near_kernel(group, chip, by_x, near):
    def first():
        in_order(group.bit(1), near, chip, by_x)

    def second():
        near[...] = chip[...]

    when(group.bit(0), second, first)


def four_kernel(group, wide, close, near, four, to_y, sent):
    def first():
        in_order(group.bit(1), sent, close, wide)
        in_order(group.bit(2), four, near, sent)
        to_y[...] = four[...]

    def second():
        for out in (four, to_y, sent):
            out[...] = wide[...]

    when(group.bit(0), second, first)


def keep_kernel(group, value, kept):
    kept[...] = value[...]


def own_kernel(group, mine, other, chip, close, by_x, sent, crossed, w, after, wp, before, far):
    def first():
        far[...] = sent[...]

        def late():
            before[...] = mul(mine[...], by_x[...])
            after[...] = other[...]

        def early():
            before[...] = mine[...]
            after[...] = mul(by_x[...], other[...])

        when(group.bit(1), late, early)

    def second():
        far[...] = crossed[...]

        def late():
            before[...] = mul(chip[...], close[...])
            row = lax.broadcasted_iota(jnp.int32, after.shape, 0)
            column = lax.broadcasted_iota(jnp.int32, after.shape, 1)
            after[...] = jnp.where(row == column, 1.0, 0.0)

        def early():
            before[...] = chip[...]
            after[...] = close[...]

        when(group.bit(1), late, early)

    when(group.bit(0), second, first)

    def late():
        before[...] = mul(before[...], far[...])

    def early():
        after[...] = mul(far[...], after[...])

    when(group.bit(2), late, early)
    wp[...] = mul(w[...], before[...])


def raw_kernel(group, wide, crossed, raw):
    def first():
        raw[...] = crossed[...]

    def second():
        raw[...] = wide[...]

    when(group.bit(0), second, first)


def opposite_near_kernel(group, raw, come, near):
    in_order(group.bit(1) == group.bit(0), near, raw, come)


def sides_kernel(group, after, wp, near, by_d, by_y, a, b, three, held):
    second, near_left, odd, upper = jnp.logical_not(group.bit(0)), group.bit(2), group.bit(3), group.bit(4)

    def four_side():
        two, one = by_d, by_y

        @pl.when(jnp.logical_not(odd))
        def _():
            held[...] = mul(one[...], after[...])

        def early():
            def odd_four():
                a[...] = mul(mul(mul_tn(after[...], wp[...]), one[...]), two[...])

            def even_four():
                a[...] = mul_tn(held[...], wp[...])
                b[...] = two[...]

            when(odd, odd_four, even_four)

            def left():
                a[...] = mul(a[...], near[...])

            def right():
                def odd_four():
                    b[...] = near[...]

                def even_four():
                    b[...] = mul(near[...], two[...])

                when(odd, odd_four, even_four)

            when(near_left, left, right)

        def late():
            def odd_four():
                a[...] = after[...].T
                b[...] = mul_tn(two[...], mul(wp[...], one[...]))

            def even_four():
                a[...] = mul(two[...], held[...]).T
                b[...] = wp[...]

            when(odd, odd_four, even_four)

            def right():
                b[...] = mul_tn(near[...], b[...])

            def left():
                a[...] = mul_nt(a[...], near[...])

            when(near_left, right, left)

        when(upper, early, late)

    def opposite_side():
        in_order(group.bit(1), held, by_y, by_d)
        in_order(near_left, three, near, held)

        def early():
            def odd_four():
                a[...] = mul_tn(after[...], wp[...])
                b[...] = three[...]

            def even_four():
                a[...] = after[...].T
                b[...] = mul(wp[...], three[...])

            when(odd, odd_four, even_four)

        def late():
            def odd_four():
                a[...] = mul(three[...], after[...]).T
                b[...] = wp[...]

            def even_four():
                a[...] = after[...].T
                b[...] = mul_tn(three[...], wp[...])

            when(odd, odd_four, even_four)

        when(upper, early, late)

    when(second, four_side, opposite_side)


def closer_kernel(group, a, b, come, new_a, new_b):
    first, x_bit, near_left, odd, upper = (group.bit(k) for k in range(5))
    second = jnp.logical_not(first)
    new_a[...] = a[...]
    new_b[...] = b[...]

    def four_side():
        def early():
            def right():
                def alone():
                    new_b[...] = come[...]

                def beside():
                    new_b[...] = mul(come[...], b[...])

                when(odd & near_left, alone, beside)

            def left():
                new_a[...] = mul(a[...], come[...])

            when(x_bit, right, left)

        def late():
            def left():
                new_a[...] = mul_nt(a[...], come[...])

            def right():
                new_b[...] = mul_tn(come[...], b[...])

            when(x_bit, left, right)

        when(upper, early, late)

    def opposite_side():
        def early():
            in_order(odd, new_b, come, b)

        def late():
            def odd_four():
                new_a[...] = mul(mul_nt(a[...], come[...]), b[...])

            def even_four():
                new_b[...] = mul_tn(come[...], b[...])

            when(odd, odd_four, even_four)

        when(upper, early, late)

    when(second, four_side, opposite_side)


def result_kernel(group, a, b, come, result, mid):
    first, x_bit, near_left, odd, upper = (group.bit(k) for k in range(5))
    second = jnp.logical_not(first)
    plain = jnp.where(second, upper, odd)
    alone = odd & jnp.where(second, upper & near_left & jnp.logical_not(x_bit), jnp.logical_not(upper))

    def as_is():
        mid[...] = mul(a[...], come[...])

    def transposed():
        mid[...] = mul_nt(a[...], come[...])

    when(plain, as_is, transposed)

    def last():
        result[...] = mid[...]

    def one_more():
        result[...] = mul(mid[...], b[...])

    when(alone, last, one_more)


def join(group, b, by, wp, after):
    flag = group.bit(b)
    new = dot(jnp.where(flag, wp, by), jnp.where(flag, by, after))
    return jnp.where(flag, new, wp), jnp.where(flag, after, new)


def pairwise(group, bits, total, wp, after):
    for b in bits:
        by = group.swap(total, 1 << b)
        wp, after = join(group, b, by, wp, after)
        total = dot(*ordered(group.bit(b), total, by))
    return dot(after.T, wp)


def body(n_in, n_out, slices, weight):
    group = Group(n_in, n_out)
    mine, w = slices[0, 0], weight[0, 0]
    square = mine.shape
    bits = group.n.bit_length() - 1
    if bits < 5:
        return pairwise(group, range(bits), mine, dot(w, mine), jnp.eye(square[0], dtype=jnp.float32))[None, None]
    other = group.swap(mine, 1)
    mine = lax.optimization_barrier(jnp.where(lax.axis_index("inner") < n_in, mine, 0.0))
    (chip,) = run(chip_kernel, group, [square], mine, other)
    by_x, wide = group.send(chip, 2, 4), group.send(chip, 6, 24)
    wide, close = lax.optimization_barrier((wide, group.swap(by_x, 1)))
    (near,) = run(near_kernel, group, [square], chip, by_x)
    four, to_y, sent = run(four_kernel, group, [square] * 3, wide, close, near)
    crossed, by_d, far_y = group.send(sent, 1, 3), group.send(four, 16, 6), group.send(to_y, 8, 4)
    after, wp = run(
        own_kernel,
        group,
        [square] * 2,
        *(mine, other, chip, close, by_x, sent, crossed, w),
        scratch=[square] * 2,
        weight=3,
    )
    crossed, after, wp = lax.optimization_barrier((crossed, after, wp))
    (raw,) = run(raw_kernel, group, [square], wide, crossed)
    (near,) = run(opposite_near_kernel, group, [square], raw, group.swap(raw, 1))
    their_d = group.swap(by_d, 1)
    by_y, by_d = lax.optimization_barrier((far_y, *run(keep_kernel, group, [square], by_d)))
    their_y = group.swap(by_y, 1)
    if bits > 5:
        second = jnp.logical_not(group.bit(0))
        one, two = jnp.where(second, by_y, their_y), jnp.where(second, by_d, their_d)
        far = dot(*ordered(group.bit(1), jnp.where(second, their_y, by_y), jnp.where(second, their_d, by_d)))
        three = dot(*ordered(group.bit(2), near, far))
        four = jnp.where(second, four, group.swap(four, 1))
        eight = dot(*ordered(group.bit(3), four, one))
        others = dot(*ordered(group.bit(3), two, three))
        wp, after = join(group, 3, one, wp, after)
        wp, after = join(group, 4, others, wp, after)
        total = dot(*ordered(group.bit(4), eight, others))
        return pairwise(group, range(5, bits), total, wp, after)[None, None]
    a, b = run(
        sides_kernel, group, [square] * 2, after, wp, near, by_d, by_y, scratch=[square] * 2, weight=4
    )
    a, b = run(closer_kernel, group, [square] * 2, a, b, their_d)
    (result,) = run(result_kernel, group, [square], a, b, their_y, scratch=[square], weight=2)
    return result[None, None]


def solution(mesh):
    spec = P("outer", "inner", None, None)
    n_in, n_out = mesh.shape["inner"], mesh.shape["outer"]

    def gradient(slices, weight):
        return body(n_in, n_out, slices, weight)

    return jax.shard_map(gradient, mesh=mesh, in_specs=(spec, spec), out_specs=spec, check_vma=False)
```

```python
import functools

import jax
import jax.numpy as jnp
from jax import lax
from jax.experimental import pallas as pl
from jax.experimental.pallas import tpu as pltpu
from jax.sharding import PartitionSpec as P


def halves(value):
    high = value.astype(jnp.bfloat16)
    return high, (value - high.astype(jnp.float32)).astype(jnp.bfloat16)


def product(left, right, dims):
    def one_pass(a, b):
        return lax.dot_general(a, b, (dims, ((), ())), preferred_element_type=jnp.float32)

    (left_high, left_low), (right_high, right_low) = halves(left), halves(right)
    cross = one_pass(left_high, right_low) + one_pass(left_low, right_high)
    return one_pass(left_high, right_high) + cross


def mul(left, right):
    return product(left, right, ((1,), (0,)))


def mul_nt(left, right):
    return product(left, right, ((1,), (1,)))


def mul_tn(left, right):
    return product(left.T, right, ((1,), (0,)))


def dot(left, right):
    return jnp.dot(left, right, precision=lax.Precision.HIGHEST, preferred_element_type=jnp.float32)


def ordered(first, a, b):
    return jnp.where(first, a, b), jnp.where(first, b, a)


class Group:
    def __init__(self, n_in, n_out):
        self.n_in, self.n = n_in, n_in * n_out
        self.place = [(k % n_in) * n_out + k // n_in for k in range(self.n)]

    def bit(self, b):
        return ((lax.axis_index("outer") * self.n_in + lax.axis_index("inner")) >> b) & 1 == 1

    def send(self, value, even, odd):
        pairs = [(self.place[k], self.place[k ^ (odd if k & 1 else even)]) for k in range(self.n)]
        return lax.ppermute(value, ("inner", "outer"), pairs)

    def swap(self, value, mask):
        return self.send(value, mask, mask)


def run(body, group, shapes, *operands, scratch=(), weight=1):
    order = operands[0].shape[-1]
    whole = pl.BlockSpec(memory_space=pltpu.VMEM)
    return pl.pallas_call(
        functools.partial(body, group),
        out_shape=[jax.ShapeDtypeStruct(shape, jnp.float32) for shape in shapes],
        in_specs=[whole] * len(operands),
        out_specs=[whole] * len(shapes),
        scratch_shapes=[pltpu.VMEM(shape, jnp.float32) for shape in scratch],
        compiler_params=pltpu.CompilerParams(vmem_limit_bytes=16 * 2**20),
        cost_estimate=pl.CostEstimate(flops=6 * weight * order**3, bytes_accessed=0, transcendentals=0),
    )(*operands)


def when(flag, then, other):
    pl.when(flag)(then)
    pl.when(jnp.logical_not(flag))(other)


def in_order(flag, out, a, b):
    def first():
        out[...] = mul(a[...], b[...])

    def last():
        out[...] = mul(b[...], a[...])

    when(flag, first, last)


def chip_kernel(group, mine, other, chip):
    in_order(group.bit(0), chip, mine, other)


def in_pieces(value, number):
    rows = value.shape[0] // number
    return [value[k * rows : (k + 1) * rows] for k in range(number)]


def near_kernel(group, chip, by_x, top, bottom, near, three, close):
    rows = top.shape[0]
    close[pl.ds(0, rows)] = top[...]
    close[pl.ds(rows, rows)] = bottom[...]

    def first():
        in_order(group.bit(1), near, chip, by_x)

        @pl.when(group.bit(1) == group.bit(2))
        def _():
            in_order(group.bit(1), three, near, close)

    def second():
        near[...] = chip[...]

    when(group.bit(0), second, first)


def four_kernel(group, wide, close, near, three, four, to_y, far):
    def first():
        def at_end():
            in_order(group.bit(1), four, three, wide)

        def inside():
            in_order(group.bit(1), far, close, wide)
            in_order(group.bit(2), four, near, far)

        when(group.bit(1) == group.bit(2), at_end, inside)
        to_y[...] = four[...]

    def second():
        four[...] = wide[...]
        to_y[...] = wide[...]

    when(group.bit(0), second, first)


def keep_kernel(group, value, kept):
    kept[...] = value[...]


def own_kernel(group, mine, other, chip, close, by_x, wide, crossed, w, after, wp, before, far):
    def first():
        in_order(group.bit(1), far, close, wide)

        def late():
            before[...] = mul(mine[...], by_x[...])
            after[...] = other[...]

        def early():
            before[...] = mine[...]
            after[...] = mul(by_x[...], other[...])

        when(group.bit(1), late, early)

    def second():
        in_order(group.bit(1), far, by_x, crossed)

        def late():
            before[...] = mul(chip[...], close[...])
            row = lax.broadcasted_iota(jnp.int32, after.shape, 0)
            column = lax.broadcasted_iota(jnp.int32, after.shape, 1)
            after[...] = jnp.where(row == column, 1.0, 0.0)

        def early():
            before[...] = chip[...]
            after[...] = close[...]

        when(group.bit(1), late, early)

    when(group.bit(0), second, first)

    def late():
        before[...] = mul(before[...], far[...])

    def early():
        after[...] = mul(far[...], after[...])

    when(group.bit(2), late, early)
    wp[...] = mul(w[...], before[...])


def raw_kernel(group, wide, crossed, raw):
    def first():
        raw[...] = crossed[...]

    def second():
        raw[...] = wide[...]

    when(group.bit(0), second, first)


def opposite_near_kernel(group, raw, come, near):
    in_order(group.bit(1) == group.bit(0), near, raw, come)


def sides_kernel(group, after, wp, near, by_d, by_y, a, b, three, held):
    second, near_left, odd, upper = jnp.logical_not(group.bit(0)), group.bit(2), group.bit(3), group.bit(4)

    def four_side():
        two, one = by_d, by_y

        @pl.when(jnp.logical_not(odd))
        def _():
            held[...] = mul(one[...], after[...])

        def early():
            def odd_four():
                a[...] = mul(mul(mul_tn(after[...], wp[...]), one[...]), two[...])

            def even_four():
                a[...] = mul_tn(held[...], wp[...])
                b[...] = two[...]

            when(odd, odd_four, even_four)

            def left():
                a[...] = mul(a[...], near[...])

            def right():
                def odd_four():
                    b[...] = near[...]

                def even_four():
                    b[...] = mul(near[...], two[...])

                when(odd, odd_four, even_four)

            when(near_left, left, right)

        def late():
            def odd_four():
                a[...] = after[...].T
                b[...] = mul_tn(two[...], mul(wp[...], one[...]))

            def even_four():
                a[...] = mul(two[...], held[...]).T
                b[...] = wp[...]

            when(odd, odd_four, even_four)

            def right():
                b[...] = mul_tn(near[...], b[...])

            def left():
                a[...] = mul_nt(a[...], near[...])

            when(near_left, right, left)

        when(upper, early, late)

    def opposite_side():
        in_order(group.bit(1), held, by_y, by_d)
        in_order(near_left, three, near, held)

        def early():
            def odd_four():
                a[...] = mul_tn(after[...], wp[...])
                b[...] = three[...]

            def even_four():
                a[...] = after[...].T
                b[...] = mul(wp[...], three[...])

            when(odd, odd_four, even_four)

        def late():
            def odd_four():
                a[...] = mul(three[...], after[...]).T
                b[...] = wp[...]

            def even_four():
                a[...] = after[...].T
                b[...] = mul_tn(three[...], wp[...])

            when(odd, odd_four, even_four)

        when(upper, early, late)

    when(second, four_side, opposite_side)


def closer_kernel(group, a, b, come, new_a, new_b):
    first, x_bit, near_left, odd, upper = (group.bit(k) for k in range(5))
    second = jnp.logical_not(first)
    new_a[...] = a[...]
    new_b[...] = b[...]

    def four_side():
        def early():
            def right():
                def alone():
                    new_b[...] = come[...]

                def beside():
                    new_b[...] = mul(come[...], b[...])

                when(odd & near_left, alone, beside)

            def left():
                new_a[...] = mul(a[...], come[...])

            when(x_bit, right, left)

        def late():
            def left():
                new_a[...] = mul_nt(a[...], come[...])

            def right():
                new_b[...] = mul_tn(come[...], b[...])

            when(x_bit, left, right)

        when(upper, early, late)

    def opposite_side():
        def early():
            in_order(odd, new_b, come, b)

        def late():
            def odd_four():
                new_a[...] = mul(mul_nt(a[...], come[...]), b[...])

            def even_four():
                new_b[...] = mul_tn(come[...], b[...])

            when(odd, odd_four, even_four)

        when(upper, early, late)

    when(second, four_side, opposite_side)


def result_kernel(group, a, b, come, result, mid):
    first, x_bit, near_left, odd, upper = (group.bit(k) for k in range(5))
    second = jnp.logical_not(first)
    plain = jnp.where(second, upper, odd)
    alone = odd & jnp.where(second, upper & near_left & jnp.logical_not(x_bit), jnp.logical_not(upper))

    def as_is():
        mid[...] = mul(a[...], come[...])

    def transposed():
        mid[...] = mul_nt(a[...], come[...])

    when(plain, as_is, transposed)

    def last():
        result[...] = mid[...]

    def one_more():
        result[...] = mul(mid[...], b[...])

    when(alone, last, one_more)


def join(group, b, by, wp, after):
    flag = group.bit(b)
    new = dot(jnp.where(flag, wp, by), jnp.where(flag, by, after))
    return jnp.where(flag, new, wp), jnp.where(flag, after, new)


def pairwise(group, bits, total, wp, after):
    for b in bits:
        by = group.swap(total, 1 << b)
        wp, after = join(group, b, by, wp, after)
        total = dot(*ordered(group.bit(b), total, by))
    return dot(after.T, wp)


def body(n_in, n_out, slices, weight):
    group = Group(n_in, n_out)
    mine, w = slices[0, 0], weight[0, 0]
    square = mine.shape
    bits = group.n.bit_length() - 1
    if bits < 5:
        return pairwise(group, range(bits), mine, dot(w, mine), jnp.eye(square[0], dtype=jnp.float32))[None, None]
    other = group.swap(mine, 1)
    mine = lax.optimization_barrier(jnp.where(lax.axis_index("inner") < n_in, mine, 0.0))
    (chip,) = run(chip_kernel, group, [square], mine, other)
    by_x, wide = group.send(chip, 2, 4), group.send(chip, 6, 24)
    pieces = [group.swap(piece, 1) for piece in in_pieces(by_x, 2)]
    near, three, close = run(near_kernel, group, [square] * 3, chip, by_x, *pieces)
    wide, near, three, close = lax.optimization_barrier((wide, near, three, close))
    crossed = group.send(wide, 1, 3)
    four, to_y = run(four_kernel, group, [square] * 2, wide, close, near, three, scratch=[square])
    by_d, far_y = group.send(four, 16, 6), group.send(to_y, 8, 4)
    after, wp = run(
        own_kernel,
        group,
        [square] * 2,
        *(mine, other, chip, close, by_x, wide, crossed, w),
        scratch=[square] * 2,
        weight=3,
    )
    crossed, after, wp = lax.optimization_barrier((crossed, after, wp))
    (raw,) = run(raw_kernel, group, [square], wide, crossed)
    (near,) = run(opposite_near_kernel, group, [square], raw, group.swap(raw, 1))
    their_d = group.swap(by_d, 1)
    by_y, by_d = lax.optimization_barrier((far_y, *run(keep_kernel, group, [square], by_d)))
    their_y = group.swap(by_y, 1)
    if bits > 5:
        second = jnp.logical_not(group.bit(0))
        one, two = jnp.where(second, by_y, their_y), jnp.where(second, by_d, their_d)
        far = dot(*ordered(group.bit(1), jnp.where(second, their_y, by_y), jnp.where(second, their_d, by_d)))
        three = dot(*ordered(group.bit(2), near, far))
        four = jnp.where(second, four, group.swap(four, 1))
        eight = dot(*ordered(group.bit(3), four, one))
        others = dot(*ordered(group.bit(3), two, three))
        wp, after = join(group, 3, one, wp, after)
        wp, after = join(group, 4, others, wp, after)
        total = dot(*ordered(group.bit(4), eight, others))
        return pairwise(group, range(5, bits), total, wp, after)[None, None]
    a, b = run(
        sides_kernel, group, [square] * 2, after, wp, near, by_d, by_y, scratch=[square] * 2, weight=4
    )
    a, b = run(closer_kernel, group, [square] * 2, a, b, their_d)
    (result,) = run(result_kernel, group, [square], a, b, their_y, scratch=[square], weight=2)
    return result[None, None]


def solution(mesh):
    spec = P("outer", "inner", None, None)
    n_in, n_out = mesh.shape["inner"], mesh.shape["outer"]

    def gradient(slices, weight):
        return body(n_in, n_out, slices, weight)

    return jax.shard_map(gradient, mesh=mesh, in_specs=(spec, spec), out_specs=spec, check_vma=False)
```

```python
import functools

import jax
import jax.numpy as jnp
from jax import lax
from jax.experimental import pallas as pl
from jax.experimental.pallas import tpu as pltpu
from jax.sharding import PartitionSpec as P


def halves(value):
    high = value.astype(jnp.bfloat16)
    return high, (value - high.astype(jnp.float32)).astype(jnp.bfloat16)


def product(left, right, dims):
    def one_pass(a, b):
        return lax.dot_general(a, b, (dims, ((), ())), preferred_element_type=jnp.float32)

    (left_high, left_low), (right_high, right_low) = halves(left), halves(right)
    cross = one_pass(left_high, right_low) + one_pass(left_low, right_high)
    return one_pass(left_high, right_high) + cross


def mul(left, right):
    return product(left, right, ((1,), (0,)))


def mul_nt(left, right):
    return product(left, right, ((1,), (1,)))


def mul_tn(left, right):
    return product(left.T, right, ((1,), (0,)))


def dot(left, right):
    return jnp.dot(left, right, precision=lax.Precision.HIGHEST, preferred_element_type=jnp.float32)


def ordered(first, a, b):
    return jnp.where(first, a, b), jnp.where(first, b, a)


class Group:
    def __init__(self, n_in, n_out):
        self.n_in, self.n = n_in, n_in * n_out
        self.place = [(k % n_in) * n_out + k // n_in for k in range(self.n)]

    def bit(self, b):
        return ((lax.axis_index("outer") * self.n_in + lax.axis_index("inner")) >> b) & 1 == 1

    def send(self, value, even, odd):
        pairs = [(self.place[k], self.place[k ^ (odd if k & 1 else even)]) for k in range(self.n)]
        return lax.ppermute(value, ("inner", "outer"), pairs)

    def swap(self, value, mask):
        return self.send(value, mask, mask)


def run(body, group, shapes, *operands, scratch=(), weight=1):
    order = operands[0].shape[-1]
    whole = pl.BlockSpec(memory_space=pltpu.VMEM)
    return pl.pallas_call(
        functools.partial(body, group),
        out_shape=[jax.ShapeDtypeStruct(shape, jnp.float32) for shape in shapes],
        in_specs=[whole] * len(operands),
        out_specs=[whole] * len(shapes),
        scratch_shapes=[pltpu.VMEM(shape, jnp.float32) for shape in scratch],
        compiler_params=pltpu.CompilerParams(vmem_limit_bytes=16 * 2**20),
        cost_estimate=pl.CostEstimate(flops=6 * weight * order**3, bytes_accessed=0, transcendentals=0),
    )(*operands)


def when(flag, then, other):
    pl.when(flag)(then)
    pl.when(jnp.logical_not(flag))(other)


def in_order(flag, out, a, b):
    def first():
        out[...] = mul(a[...], b[...])

    def last():
        out[...] = mul(b[...], a[...])

    when(flag, first, last)


def chip_kernel(group, mine, other, chip):
    in_order(group.bit(0), chip, mine, other)


def in_pieces(value, number):
    rows = value.shape[0] // number
    return [value[k * rows : (k + 1) * rows] for k in range(number)]


def near_kernel(group, chip, by_x, top, bottom, near, three, close):
    rows = top.shape[0]
    close[pl.ds(0, rows)] = top[...]
    close[pl.ds(rows, rows)] = bottom[...]

    def first():
        in_order(group.bit(1), near, chip, by_x)

        @pl.when(group.bit(1) == group.bit(2))
        def _():
            in_order(group.bit(1), three, near, close)

    def second():
        near[...] = chip[...]

    when(group.bit(0), second, first)


def four_kernel(group, wide, close, near, three, four, to_y, far):
    def first():
        def at_end():
            in_order(group.bit(1), four, three, wide)

        def inside():
            in_order(group.bit(1), far, close, wide)
            in_order(group.bit(2), four, near, far)

        when(group.bit(1) == group.bit(2), at_end, inside)
        to_y[...] = four[...]

    def second():
        four[...] = wide[...]
        to_y[...] = wide[...]

    when(group.bit(0), second, first)


def keep_kernel(group, value, kept):
    kept[...] = value[...]


def own_kernel(group, mine, other, chip, close, by_x, wide, crossed, w, after, wp, before, far):
    def first():
        in_order(group.bit(1), far, close, wide)

        def late():
            before[...] = mul(mine[...], by_x[...])
            after[...] = other[...]

        def early():
            before[...] = mine[...]
            after[...] = mul(by_x[...], other[...])

        when(group.bit(1), late, early)

    def second():
        in_order(group.bit(1), far, by_x, crossed)

        def late():
            before[...] = mul(chip[...], close[...])
            row = lax.broadcasted_iota(jnp.int32, after.shape, 0)
            column = lax.broadcasted_iota(jnp.int32, after.shape, 1)
            after[...] = jnp.where(row == column, 1.0, 0.0)

        def early():
            before[...] = chip[...]
            after[...] = close[...]

        when(group.bit(1), late, early)

    when(group.bit(0), second, first)

    def late():
        before[...] = mul(before[...], far[...])

    def early():
        after[...] = mul(far[...], after[...])

    when(group.bit(2), late, early)
    wp[...] = mul(w[...], before[...])


def raw_kernel(group, wide, crossed, top, bottom):
    rows = top.shape[0]

    def send(value):
        top[...] = value[pl.ds(0, rows)]
        bottom[...] = value[pl.ds(rows, rows)]

    when(group.bit(0), lambda: send(wide), lambda: send(crossed))


def opposite_near_kernel(group, crossed, top, bottom, near):
    rows = top.shape[0]
    near[pl.ds(0, rows)] = top[...]
    near[pl.ds(rows, rows)] = bottom[...]

    @pl.when(jnp.logical_not(group.bit(0)))
    def _():
        left = jnp.where(group.bit(1), near[...], crossed[...])
        right = jnp.where(group.bit(1), crossed[...], near[...])
        near[...] = mul(left, right)


def sides_kernel(group, after, wp, near, wide, by_d, by_y, a, b, three, held, opposite):
    second, near_left, odd, upper = jnp.logical_not(group.bit(0)), group.bit(2), group.bit(3), group.bit(4)

    def four_side():
        two, one = by_d, by_y

        @pl.when(jnp.logical_not(odd))
        def _():
            held[...] = mul(one[...], after[...])

        def early():
            def odd_four():
                a[...] = mul(mul(mul_tn(after[...], wp[...]), one[...]), two[...])

            def even_four():
                a[...] = mul_tn(held[...], wp[...])
                b[...] = two[...]

            when(odd, odd_four, even_four)

            def left():
                a[...] = mul(a[...], near[...])

            def right():
                def odd_four():
                    b[...] = near[...]

                def even_four():
                    b[...] = mul(near[...], two[...])

                when(odd, odd_four, even_four)

            when(near_left, left, right)

        def late():
            def odd_four():
                a[...] = after[...].T
                b[...] = mul_tn(two[...], mul(wp[...], one[...]))

            def even_four():
                a[...] = mul(two[...], held[...]).T
                b[...] = wp[...]

            when(odd, odd_four, even_four)

            def right():
                b[...] = mul_tn(near[...], b[...])

            def left():
                a[...] = mul_nt(a[...], near[...])

            when(near_left, right, left)

        when(upper, early, late)

    def opposite_side():
        in_order(group.bit(1), held, by_d, by_y)
        in_order(group.bit(1), opposite, wide, near)
        in_order(near_left, three, opposite, held)

        def early():
            def odd_four():
                a[...] = mul_tn(after[...], wp[...])
                b[...] = three[...]

            def even_four():
                a[...] = after[...].T
                b[...] = mul(wp[...], three[...])

            when(odd, odd_four, even_four)

        def late():
            def odd_four():
                a[...] = mul(three[...], after[...]).T
                b[...] = wp[...]

            def even_four():
                a[...] = after[...].T
                b[...] = mul_tn(three[...], wp[...])

            when(odd, odd_four, even_four)

        when(upper, early, late)

    when(second, four_side, opposite_side)


def closer_kernel(group, a, b, come, new_a, new_b):
    first, x_bit, near_left, odd, upper = (group.bit(k) for k in range(5))
    second, x_bit = jnp.logical_not(first), jnp.logical_not(x_bit)
    new_a[...] = a[...]
    new_b[...] = b[...]

    def four_side():
        def early():
            def right():
                def alone():
                    new_b[...] = come[...]

                def beside():
                    new_b[...] = mul(come[...], b[...])

                when(odd & near_left, alone, beside)

            def left():
                new_a[...] = mul(a[...], come[...])

            when(x_bit, right, left)

        def late():
            def left():
                new_a[...] = mul_nt(a[...], come[...])

            def right():
                new_b[...] = mul_tn(come[...], b[...])

            when(x_bit, left, right)

        when(upper, early, late)

    def opposite_side():
        def early():
            in_order(odd, new_b, come, b)

        def late():
            def odd_four():
                new_a[...] = mul(mul_nt(a[...], come[...]), b[...])

            def even_four():
                new_b[...] = mul_tn(come[...], b[...])

            when(odd, odd_four, even_four)

        when(upper, early, late)

    when(second, four_side, opposite_side)


def result_kernel(group, a, b, come, result, mid):
    first, x_bit, near_left, odd, upper = (group.bit(k) for k in range(5))
    second, x_bit = jnp.logical_not(first), jnp.logical_not(x_bit)
    plain = jnp.where(second, upper, odd)
    alone = odd & jnp.where(second, upper & near_left & jnp.logical_not(x_bit), jnp.logical_not(upper))

    def as_is():
        mid[...] = mul(a[...], come[...])

    def transposed():
        mid[...] = mul_nt(a[...], come[...])

    when(plain, as_is, transposed)

    def last():
        result[...] = mid[...]

    def one_more():
        result[...] = mul(mid[...], b[...])

    when(alone, last, one_more)


def join(group, b, by, wp, after):
    flag = group.bit(b)
    new = dot(jnp.where(flag, wp, by), jnp.where(flag, by, after))
    return jnp.where(flag, new, wp), jnp.where(flag, after, new)


def pairwise(group, bits, total, wp, after):
    for b in bits:
        by = group.swap(total, 1 << b)
        wp, after = join(group, b, by, wp, after)
        total = dot(*ordered(group.bit(b), total, by))
    return dot(after.T, wp)


def body(n_in, n_out, slices, weight):
    group = Group(n_in, n_out)
    mine, w = slices[0, 0], weight[0, 0]
    square = mine.shape
    bits = group.n.bit_length() - 1
    if bits < 5:
        return pairwise(group, range(bits), mine, dot(w, mine), jnp.eye(square[0], dtype=jnp.float32))[None, None]
    other = group.swap(mine, 1)
    mine = lax.optimization_barrier(jnp.where(lax.axis_index("inner") < n_in, mine, 0.0))
    (chip,) = run(chip_kernel, group, [square], mine, other)
    by_x, wide = group.send(chip, 2, 4), group.send(chip, 6, 24)
    pieces = [group.swap(piece, 1) for piece in in_pieces(by_x, 2)]
    near, three, close = run(near_kernel, group, [square] * 3, chip, by_x, *pieces)
    wide, near, three, close = lax.optimization_barrier((wide, near, three, close))
    crossed = group.send(wide, 1, 3)
    four, to_y = run(four_kernel, group, [square] * 2, wide, close, near, three, scratch=[square])
    by_d, far_y = group.send(four, 16, 4), group.send(to_y, 8, 6)
    after, wp = run(
        own_kernel,
        group,
        [square] * 2,
        *(mine, other, chip, close, by_x, wide, crossed, w),
        scratch=[square] * 2,
        weight=3,
    )
    crossed, after, wp = lax.optimization_barrier((crossed, after, wp))
    half = (square[0] // 2, square[1])
    pieces = [group.swap(piece, 1) for piece in run(raw_kernel, group, [half] * 2, wide, crossed)]
    (near,) = run(opposite_near_kernel, group, [square], crossed, *pieces)
    their_d = group.swap(by_d, 1)
    by_y, by_d, near = lax.optimization_barrier((far_y, *run(keep_kernel, group, [square], by_d), near))
    their_y = group.swap(by_y, 1)
    if bits > 5:
        second = jnp.logical_not(group.bit(0))
        one, two = jnp.where(second, by_y, their_y), jnp.where(second, by_d, their_d)
        far = dot(*ordered(group.bit(1), jnp.where(second, their_d, by_d), jnp.where(second, their_y, by_y)))
        near = jnp.where(second, near, dot(*ordered(group.bit(1), wide, near)))
        three = dot(*ordered(group.bit(2), near, far))
        four = jnp.where(second, four, group.swap(four, 1))
        eight = dot(*ordered(group.bit(3), four, one))
        others = dot(*ordered(group.bit(3), two, three))
        wp, after = join(group, 3, one, wp, after)
        wp, after = join(group, 4, others, wp, after)
        total = dot(*ordered(group.bit(4), eight, others))
        return pairwise(group, range(5, bits), total, wp, after)[None, None]
    a, b = run(
        sides_kernel, group, [square] * 2, after, wp, near, wide, by_d, by_y, scratch=[square] * 3, weight=4
    )
    a, b = run(closer_kernel, group, [square] * 2, a, b, their_d)
    (result,) = run(result_kernel, group, [square], a, b, their_y, scratch=[square], weight=2)
    return result[None, None]


def solution(mesh):
    spec = P("outer", "inner", None, None)
    n_in, n_out = mesh.shape["inner"], mesh.shape["outer"]

    def gradient(slices, weight):
        return body(n_in, n_out, slices, weight)

    return jax.shard_map(gradient, mesh=mesh, in_specs=(spec, spec), out_specs=spec, check_vma=False)
```

```python
import functools

import jax
import jax.numpy as jnp
from jax import lax
from jax.experimental import pallas as pl
from jax.experimental.pallas import tpu as pltpu
from jax.sharding import PartitionSpec as P


def halves(value):
    high = value.astype(jnp.bfloat16)
    return high, (value - high.astype(jnp.float32)).astype(jnp.bfloat16)


def product(left, right, dims):
    def one_pass(a, b):
        return lax.dot_general(a, b, (dims, ((), ())), preferred_element_type=jnp.float32)

    (left_high, left_low), (right_high, right_low) = halves(left), halves(right)
    cross = one_pass(left_high, right_low) + one_pass(left_low, right_high)
    return one_pass(left_high, right_high) + cross


def mul(left, right):
    return product(left, right, ((1,), (0,)))


def mul_nt(left, right):
    return product(left, right, ((1,), (1,)))


def mul_tn(left, right):
    return product(left.T, right, ((1,), (0,)))


def dot(left, right):
    return jnp.dot(left, right, precision=lax.Precision.HIGHEST, preferred_element_type=jnp.float32)


def ordered(first, a, b):
    return jnp.where(first, a, b), jnp.where(first, b, a)


class Group:
    def __init__(self, n_in, n_out):
        self.n_in, self.n = n_in, n_in * n_out
        self.place = [(k % n_in) * n_out + k // n_in for k in range(self.n)]

    def bit(self, b):
        return ((lax.axis_index("outer") * self.n_in + lax.axis_index("inner")) >> b) & 1 == 1

    def send(self, value, even, odd):
        pairs = [(self.place[k], self.place[k ^ (odd if k & 1 else even)]) for k in range(self.n)]
        return lax.ppermute(value, ("inner", "outer"), pairs)

    def swap(self, value, mask):
        return self.send(value, mask, mask)


def run(body, group, shapes, *operands, scratch=(), weight=1):
    order = operands[0].shape[-1]
    whole = pl.BlockSpec(memory_space=pltpu.VMEM)
    return pl.pallas_call(
        functools.partial(body, group),
        out_shape=[jax.ShapeDtypeStruct(shape, jnp.float32) for shape in shapes],
        in_specs=[whole] * len(operands),
        out_specs=[whole] * len(shapes),
        scratch_shapes=[pltpu.VMEM(shape, jnp.float32) for shape in scratch],
        compiler_params=pltpu.CompilerParams(vmem_limit_bytes=16 * 2**20),
        cost_estimate=pl.CostEstimate(flops=6 * weight * order**3, bytes_accessed=0, transcendentals=0),
    )(*operands)


def when(flag, then, other):
    pl.when(flag)(then)
    pl.when(jnp.logical_not(flag))(other)


def in_order(flag, out, a, b):
    def first():
        out[...] = mul(a[...], b[...])

    def last():
        out[...] = mul(b[...], a[...])

    when(flag, first, last)


def chip_kernel(group, mine, other, chip):
    in_order(group.bit(0), chip, mine, other)


def in_pieces(value, number):
    rows = value.shape[0] // number
    return [value[k * rows : (k + 1) * rows] for k in range(number)]


def near_kernel(group, chip, by_x, top, bottom, near, three, close):
    rows = top.shape[0]
    close[pl.ds(0, rows)] = top[...]
    close[pl.ds(rows, rows)] = bottom[...]

    def first():
        in_order(group.bit(1), near, chip, by_x)

        @pl.when(group.bit(1) == group.bit(2))
        def _():
            in_order(group.bit(1), three, near, close)

    def second():
        near[...] = chip[...]

    when(group.bit(0), second, first)


def four_kernel(group, wide, close, near, three, four, to_y, far):
    def first():
        def at_end():
            in_order(group.bit(1), four, three, wide)

        def inside():
            in_order(group.bit(1), far, close, wide)
            in_order(group.bit(2), four, near, far)

        when(group.bit(1) == group.bit(2), at_end, inside)
        to_y[...] = four[...]

    def second():
        four[...] = wide[...]
        to_y[...] = wide[...]

    when(group.bit(0), second, first)


def keep_kernel(group, value, kept):
    kept[...] = value[...]


def own_kernel(group, mine, other, chip, close, by_x, wide, crossed, w, after, wp, before, far):
    def first():
        in_order(group.bit(1), far, close, wide)

        def late():
            before[...] = mul(mine[...], by_x[...])
            after[...] = other[...]

        def early():
            before[...] = mine[...]
            after[...] = mul(by_x[...], other[...])

        when(group.bit(1), late, early)

    def second():
        in_order(group.bit(1), far, by_x, crossed)

        def late():
            before[...] = mul(chip[...], close[...])
            row = lax.broadcasted_iota(jnp.int32, after.shape, 0)
            column = lax.broadcasted_iota(jnp.int32, after.shape, 1)
            after[...] = jnp.where(row == column, 1.0, 0.0)

        def early():
            before[...] = chip[...]
            after[...] = close[...]

        when(group.bit(1), late, early)

    when(group.bit(0), second, first)

    def late():
        before[...] = mul(before[...], far[...])

    def early():
        after[...] = mul(far[...], after[...])

    when(group.bit(2), late, early)
    wp[...] = mul(w[...], before[...])


def raw_kernel(group, wide, crossed, top, bottom):
    rows = top.shape[0]

    def send(value):
        top[...] = value[pl.ds(0, rows)]
        bottom[...] = value[pl.ds(rows, rows)]

    when(group.bit(0), lambda: send(wide), lambda: send(crossed))


def opposite_near_kernel(group, crossed, top, bottom, near):
    rows = top.shape[0]
    near[pl.ds(0, rows)] = top[...]
    near[pl.ds(rows, rows)] = bottom[...]

    @pl.when(jnp.logical_not(group.bit(0)))
    def _():
        left = jnp.where(group.bit(1), near[...], crossed[...])
        right = jnp.where(group.bit(1), crossed[...], near[...])
        near[...] = mul(left, right)


def sides_kernel(group, after, wp, near, wide, by_d, by_y, a, b, three, held, opposite):
    second, near_left, odd, upper = jnp.logical_not(group.bit(0)), group.bit(2), group.bit(3), group.bit(4)

    def four_side():
        two, one = by_d, by_y

        @pl.when(jnp.logical_not(odd) & (upper | near_left))
        def _():
            held[...] = mul(one[...], after[...])

        def early():
            def odd_four():
                a[...] = mul(mul(mul_tn(after[...], wp[...]), one[...]), two[...])

            def even_four():
                a[...] = mul_tn(held[...], wp[...])
                b[...] = two[...]

            when(odd, odd_four, even_four)

            def left():
                a[...] = mul(a[...], near[...])

            def right():
                def odd_four():
                    b[...] = near[...]

                def even_four():
                    b[...] = mul(near[...], two[...])

                when(odd, odd_four, even_four)

            when(near_left, left, right)

        def late():
            def right():
                b[...] = mul_tn(near[...], b[...])

            def left():
                a[...] = mul_nt(a[...], near[...])

            def odd_four():
                a[...] = after[...].T
                b[...] = mul_tn(two[...], mul(wp[...], one[...]))
                when(near_left, right, left)

            def even_right():
                b[...] = mul_tn(near[...], wp[...])
                a[...] = mul(two[...], held[...]).T

            def even_left():
                b[...] = wp[...]
                a[...] = mul(mul(near[...], two[...]), mul(one[...], after[...])).T

            def even_four():
                when(near_left, even_right, even_left)

            when(odd, odd_four, even_four)

        when(upper, early, late)

    def opposite_side():
        x_bit = group.bit(1)
        held[...] = mul(*ordered(x_bit, by_d[...], by_y[...]))
        opposite[...] = mul(*ordered(x_bit, wide[...], near[...]))
        in_order(near_left, three, opposite, held)

        def early():
            def odd_four():
                a[...] = mul_tn(after[...], wp[...])
                b[...] = three[...]

            def even_four():
                a[...] = after[...].T
                b[...] = mul(wp[...], three[...])

            when(odd, odd_four, even_four)

        def late():
            def odd_four():
                a[...] = mul(three[...], after[...]).T
                b[...] = wp[...]

            def even_four():
                a[...] = after[...].T
                b[...] = mul_tn(three[...], wp[...])

            when(odd, odd_four, even_four)

        when(upper, early, late)

    when(second, four_side, opposite_side)


def closer_kernel(group, a, b, come, new_a, new_b):
    first, x_bit, near_left, odd, upper = (group.bit(k) for k in range(5))
    second, x_bit = jnp.logical_not(first), jnp.logical_not(x_bit)
    new_a[...] = a[...]
    new_b[...] = b[...]

    def four_side():
        def early():
            def right():
                def alone():
                    new_b[...] = come[...]

                def beside():
                    new_b[...] = mul(come[...], b[...])

                when(odd & near_left, alone, beside)

            def left():
                new_a[...] = mul(a[...], come[...])

            when(x_bit, right, left)

        def late():
            def left():
                new_a[...] = mul_nt(a[...], come[...])

            def right():
                new_b[...] = mul_tn(come[...], b[...])

            when(x_bit, left, right)

        when(upper, early, late)

    def opposite_side():
        def early():
            in_order(odd, new_b, come, b)

        def late():
            def odd_four():
                new_a[...] = mul(mul_nt(a[...], come[...]), b[...])

            def even_four():
                new_b[...] = mul_tn(come[...], b[...])

            when(odd, odd_four, even_four)

        when(upper, early, late)

    when(second, four_side, opposite_side)


def result_kernel(group, a, b, come, result, mid):
    first, x_bit, near_left, odd, upper = (group.bit(k) for k in range(5))
    second, x_bit = jnp.logical_not(first), jnp.logical_not(x_bit)
    plain = jnp.where(second, upper, odd)
    alone = odd & jnp.where(second, upper & near_left & jnp.logical_not(x_bit), jnp.logical_not(upper))

    def as_is():
        mid[...] = mul(a[...], come[...])

    def transposed():
        mid[...] = mul_nt(a[...], come[...])

    when(plain, as_is, transposed)

    def last():
        result[...] = mid[...]

    def one_more():
        result[...] = mul(mid[...], b[...])

    when(alone, last, one_more)


def join(group, b, by, wp, after):
    flag = group.bit(b)
    new = dot(jnp.where(flag, wp, by), jnp.where(flag, by, after))
    return jnp.where(flag, new, wp), jnp.where(flag, after, new)


def pairwise(group, bits, total, wp, after):
    for b in bits:
        by = group.swap(total, 1 << b)
        wp, after = join(group, b, by, wp, after)
        total = dot(*ordered(group.bit(b), total, by))
    return dot(after.T, wp)


def body(n_in, n_out, slices, weight):
    group = Group(n_in, n_out)
    mine, w = slices[0, 0], weight[0, 0]
    square = mine.shape
    bits = group.n.bit_length() - 1
    if bits < 5:
        return pairwise(group, range(bits), mine, dot(w, mine), jnp.eye(square[0], dtype=jnp.float32))[None, None]
    other = group.swap(mine, 1)
    mine = lax.optimization_barrier(jnp.where(lax.axis_index("inner") < n_in, mine, 0.0))
    (chip,) = run(chip_kernel, group, [square], mine, other)
    by_x, wide = group.send(chip, 2, 4), group.send(chip, 6, 24)
    pieces = [group.swap(piece, 1) for piece in in_pieces(by_x, 2)]
    near, three, close = run(near_kernel, group, [square] * 3, chip, by_x, *pieces)
    wide, near, three, close = lax.optimization_barrier((wide, near, three, close))
    crossed = group.send(wide, 1, 3)
    four, to_y = run(four_kernel, group, [square] * 2, wide, close, near, three, scratch=[square])
    by_d, far_y = group.send(four, 16, 4), group.send(to_y, 8, 6)
    after, wp = run(
        own_kernel,
        group,
        [square] * 2,
        *(mine, other, chip, close, by_x, wide, crossed, w),
        scratch=[square] * 2,
        weight=3,
    )
    crossed, after, wp = lax.optimization_barrier((crossed, after, wp))
    half = (square[0] // 2, square[1])
    pieces = [group.swap(piece, 1) for piece in run(raw_kernel, group, [half] * 2, wide, crossed)]
    (near,) = run(opposite_near_kernel, group, [square], crossed, *pieces)
    their_d = group.swap(by_d, 1)
    by_y, by_d, near = lax.optimization_barrier((far_y, *run(keep_kernel, group, [square], by_d), near))
    their_y = group.swap(by_y, 1)
    if bits > 5:
        second = jnp.logical_not(group.bit(0))
        one, two = jnp.where(second, by_y, their_y), jnp.where(second, by_d, their_d)
        far = dot(*ordered(group.bit(1), jnp.where(second, their_d, by_d), jnp.where(second, their_y, by_y)))
        near = jnp.where(second, near, dot(*ordered(group.bit(1), wide, near)))
        three = dot(*ordered(group.bit(2), near, far))
        four = jnp.where(second, four, group.swap(four, 1))
        eight = dot(*ordered(group.bit(3), four, one))
        others = dot(*ordered(group.bit(3), two, three))
        wp, after = join(group, 3, one, wp, after)
        wp, after = join(group, 4, others, wp, after)
        total = dot(*ordered(group.bit(4), eight, others))
        return pairwise(group, range(5, bits), total, wp, after)[None, None]
    a, b = run(
        sides_kernel, group, [square] * 2, after, wp, near, wide, by_d, by_y, scratch=[square] * 3, weight=4
    )
    a, b = run(closer_kernel, group, [square] * 2, a, b, their_d)
    (result,) = run(result_kernel, group, [square], a, b, their_y, scratch=[square], weight=2)
    return result[None, None]


def solution(mesh):
    spec = P("outer", "inner", None, None)
    n_in, n_out = mesh.shape["inner"], mesh.shape["outer"]

    def gradient(slices, weight):
        return body(n_in, n_out, slices, weight)

    return jax.shard_map(gradient, mesh=mesh, in_specs=(spec, spec), out_specs=spec, check_vma=False)
```

```python
import functools

import jax
import jax.numpy as jnp
from jax import lax
from jax.experimental import pallas as pl
from jax.experimental.pallas import tpu as pltpu
from jax.sharding import PartitionSpec as P


def halves(value):
    high = value.astype(jnp.bfloat16)
    return high, (value - high.astype(jnp.float32)).astype(jnp.bfloat16)


def product(left, right, dims):
    def one_pass(a, b):
        return lax.dot_general(a, b, (dims, ((), ())), preferred_element_type=jnp.float32)

    (left_high, left_low), (right_high, right_low) = halves(left), halves(right)
    cross = one_pass(left_high, right_low) + one_pass(left_low, right_high)
    return one_pass(left_high, right_high) + cross


def mul(left, right):
    return product(left, right, ((1,), (0,)))


def mul_nt(left, right):
    return product(left, right, ((1,), (1,)))


def mul_tn(left, right):
    return product(left.T, right, ((1,), (0,)))


def dot(left, right):
    return jnp.dot(left, right, precision=lax.Precision.HIGHEST, preferred_element_type=jnp.float32)


def ordered(first, a, b):
    return jnp.where(first, a, b), jnp.where(first, b, a)


class Group:
    def __init__(self, n_in, n_out):
        self.n_in, self.n = n_in, n_in * n_out
        self.place = [(k % n_in) * n_out + k // n_in for k in range(self.n)]

    def bit(self, b):
        return ((lax.axis_index("outer") * self.n_in + lax.axis_index("inner")) >> b) & 1 == 1

    def send(self, value, even, odd):
        pairs = [(self.place[k], self.place[k ^ (odd if k & 1 else even)]) for k in range(self.n)]
        return lax.ppermute(value, ("inner", "outer"), pairs)

    def swap(self, value, mask):
        return self.send(value, mask, mask)


def run(body, group, shapes, *operands, scratch=(), weight=1):
    order = operands[0].shape[-1]
    whole = pl.BlockSpec(memory_space=pltpu.VMEM)
    return pl.pallas_call(
        functools.partial(body, group),
        out_shape=[jax.ShapeDtypeStruct(shape, jnp.float32) for shape in shapes],
        in_specs=[whole] * len(operands),
        out_specs=[whole] * len(shapes),
        scratch_shapes=[pltpu.VMEM(shape, jnp.float32) for shape in scratch],
        compiler_params=pltpu.CompilerParams(vmem_limit_bytes=16 * 2**20),
        cost_estimate=pl.CostEstimate(flops=6 * weight * order**3, bytes_accessed=0, transcendentals=0),
    )(*operands)


def when(flag, then, other):
    pl.when(flag)(then)
    pl.when(jnp.logical_not(flag))(other)


def in_order(flag, out, a, b):
    def first():
        out[...] = mul(a[...], b[...])

    def last():
        out[...] = mul(b[...], a[...])

    when(flag, first, last)


def chip_kernel(group, mine, other, chip):
    in_order(group.bit(0), chip, mine, other)


def in_pieces(value, number):
    rows = value.shape[0] // number
    return [value[k * rows : (k + 1) * rows] for k in range(number)]


def near_kernel(group, chip, by_x, top, bottom, near, three, close):
    rows = top.shape[0]
    close[pl.ds(0, rows)] = top[...]
    close[pl.ds(rows, rows)] = bottom[...]

    def first():
        in_order(group.bit(1), near, chip, by_x)

        @pl.when(group.bit(1) == group.bit(2))
        def _():
            in_order(group.bit(1), three, near, close)

    def second():
        near[...] = chip[...]

    when(group.bit(0), second, first)


def four_kernel(group, wide, close, near, three, four, to_y, far):
    def first():
        def at_end():
            in_order(group.bit(1), four, three, wide)

        def inside():
            in_order(group.bit(1), far, close, wide)
            in_order(group.bit(2), four, near, far)

        when(group.bit(1) == group.bit(2), at_end, inside)
        to_y[...] = four[...]

    def second():
        four[...] = wide[...]
        to_y[...] = wide[...]

    when(group.bit(0), second, first)


def keep_kernel(group, value, kept):
    kept[...] = value[...]


def own_kernel(group, mine, other, chip, close, by_x, wide, crossed, w, after, wp, before, far):
    def first():
        in_order(group.bit(1), far, close, wide)

        def late():
            before[...] = mul(mine[...], by_x[...])
            after[...] = other[...]

        def early():
            before[...] = mine[...]
            after[...] = mul(by_x[...], other[...])

        when(group.bit(1), late, early)

    def second():
        in_order(group.bit(1), far, by_x, crossed)

        def late():
            before[...] = mul(chip[...], close[...])
            row = lax.broadcasted_iota(jnp.int32, after.shape, 0)
            column = lax.broadcasted_iota(jnp.int32, after.shape, 1)
            after[...] = jnp.where(row == column, 1.0, 0.0)

        def early():
            before[...] = chip[...]
            after[...] = close[...]

        when(group.bit(1), late, early)

    when(group.bit(0), second, first)

    def late():
        before[...] = mul(before[...], far[...])

    def early():
        after[...] = mul(far[...], after[...])

    when(group.bit(2), late, early)
    wp[...] = mul(w[...], before[...])


def raw_kernel(group, wide, crossed, top, bottom):
    rows = top.shape[0]

    def send(value):
        top[...] = value[pl.ds(0, rows)]
        bottom[...] = value[pl.ds(rows, rows)]

    when(group.bit(0), lambda: send(wide), lambda: send(crossed))


def opposite_near_kernel(group, crossed, top, bottom, near):
    rows = top.shape[0]
    near[pl.ds(0, rows)] = top[...]
    near[pl.ds(rows, rows)] = bottom[...]

    @pl.when(jnp.logical_not(group.bit(0)))
    def _():
        left = jnp.where(group.bit(1), near[...], crossed[...])
        right = jnp.where(group.bit(1), crossed[...], near[...])
        near[...] = mul(left, right)


def sides_kernel(group, after, wp, near, wide, by_d, by_y, a, b, three, held, opposite):
    second, near_left, odd, upper = jnp.logical_not(group.bit(0)), group.bit(2), group.bit(3), group.bit(4)

    def four_side():
        two, one = by_d, by_y

        @pl.when(jnp.logical_not(odd) & (upper | near_left))
        def _():
            held[...] = mul(one[...], after[...])

        def early():
            def odd_four():
                a[...] = mul(mul(mul_tn(after[...], wp[...]), one[...]), two[...])

            def even_four():
                a[...] = mul_tn(held[...], wp[...])
                b[...] = two[...]

            when(odd, odd_four, even_four)

            def left():
                a[...] = mul(a[...], near[...])

            def right():
                def odd_four():
                    b[...] = near[...]

                def even_four():
                    b[...] = mul(near[...], two[...])

                when(odd, odd_four, even_four)

            when(near_left, left, right)

        def late():
            def right():
                b[...] = mul_tn(near[...], b[...])

            def left():
                a[...] = mul_nt(a[...], near[...])

            def odd_four():
                a[...] = after[...].T
                b[...] = mul_tn(two[...], mul(wp[...], one[...]))
                when(near_left, right, left)

            def even_right():
                b[...] = mul_tn(near[...], wp[...])
                a[...] = mul(two[...], held[...]).T

            def even_left():
                b[...] = wp[...]
                a[...] = mul(mul(near[...], two[...]), mul(one[...], after[...])).T

            def even_four():
                when(near_left, even_right, even_left)

            when(odd, odd_four, even_four)

        when(upper, early, late)

    def opposite_side():
        x_bit = group.bit(1)
        held[...] = mul(*ordered(x_bit, by_y[...], by_d[...]))
        opposite[...] = mul(*ordered(x_bit, wide[...], near[...]))
        in_order(near_left, three, opposite, held)

        def early():
            def odd_four():
                a[...] = mul_tn(after[...], wp[...])
                b[...] = three[...]

            def even_four():
                a[...] = after[...].T
                b[...] = mul(wp[...], three[...])

            when(odd, odd_four, even_four)

        def late():
            def odd_four():
                a[...] = mul(three[...], after[...]).T
                b[...] = wp[...]

            def even_four():
                a[...] = after[...].T
                b[...] = mul_tn(three[...], wp[...])

            when(odd, odd_four, even_four)

        when(upper, early, late)

    when(second, four_side, opposite_side)


def closer_kernel(group, a, b, come, new_a, new_b):
    first, x_bit, near_left, odd, upper = (group.bit(k) for k in range(5))
    second = jnp.logical_not(first)
    new_a[...] = a[...]
    new_b[...] = b[...]

    def four_side():
        def early():
            def right():
                def alone():
                    new_b[...] = come[...]

                def beside():
                    new_b[...] = mul(come[...], b[...])

                when(odd & near_left, alone, beside)

            def left():
                new_a[...] = mul(a[...], come[...])

            when(x_bit, right, left)

        def late():
            def left():
                new_a[...] = mul_nt(a[...], come[...])

            def right():
                new_b[...] = mul_tn(come[...], b[...])

            when(x_bit, left, right)

        when(upper, early, late)

    def opposite_side():
        def early():
            in_order(odd, new_b, come, b)

        def late():
            def odd_four():
                new_a[...] = mul(mul_nt(a[...], come[...]), b[...])

            def even_four():
                new_b[...] = mul_tn(come[...], b[...])

            when(odd, odd_four, even_four)

        when(upper, early, late)

    when(second, four_side, opposite_side)


def result_kernel(group, a, b, come, result, mid):
    first, x_bit, near_left, odd, upper = (group.bit(k) for k in range(5))
    second = jnp.logical_not(first)
    plain = jnp.where(second, upper, odd)
    alone = odd & jnp.where(second, upper & near_left & jnp.logical_not(x_bit), jnp.logical_not(upper))

    def as_is():
        mid[...] = mul(a[...], come[...])

    def transposed():
        mid[...] = mul_nt(a[...], come[...])

    when(plain, as_is, transposed)

    def last():
        result[...] = mid[...]

    def one_more():
        result[...] = mul(mid[...], b[...])

    when(alone, last, one_more)


def join(group, b, by, wp, after):
    flag = group.bit(b)
    new = dot(jnp.where(flag, wp, by), jnp.where(flag, by, after))
    return jnp.where(flag, new, wp), jnp.where(flag, after, new)


def pairwise(group, bits, total, wp, after):
    for b in bits:
        by = group.swap(total, 1 << b)
        wp, after = join(group, b, by, wp, after)
        total = dot(*ordered(group.bit(b), total, by))
    return dot(after.T, wp)


def body(n_in, n_out, slices, weight):
    group = Group(n_in, n_out)
    mine, w = slices[0, 0], weight[0, 0]
    square = mine.shape
    bits = group.n.bit_length() - 1
    if bits < 5:
        return pairwise(group, range(bits), mine, dot(w, mine), jnp.eye(square[0], dtype=jnp.float32))[None, None]
    other = group.swap(mine, 1)
    mine = lax.optimization_barrier(jnp.where(lax.axis_index("inner") < n_in, mine, 0.0))
    (chip,) = run(chip_kernel, group, [square], mine, other)
    by_x, wide = group.send(chip, 2, 4), group.send(chip, 6, 24)
    pieces = [group.swap(piece, 1) for piece in in_pieces(by_x, 2)]
    near, three, close = run(near_kernel, group, [square] * 3, chip, by_x, *pieces)
    wide, near, three, close = lax.optimization_barrier((wide, near, three, close))
    crossed = group.send(wide, 1, 3)
    four, to_y = run(four_kernel, group, [square] * 2, wide, close, near, three, scratch=[square])
    by_d, far_y = group.send(four, 16, 6), group.send(to_y, 8, 4)
    after, wp = run(
        own_kernel,
        group,
        [square] * 2,
        *(mine, other, chip, close, by_x, wide, crossed, w),
        scratch=[square] * 2,
        weight=3,
    )
    crossed, after, wp = lax.optimization_barrier((crossed, after, wp))
    half = (square[0] // 2, square[1])
    pieces = [group.swap(piece, 1) for piece in run(raw_kernel, group, [half] * 2, wide, crossed)]
    (near,) = run(opposite_near_kernel, group, [square], crossed, *pieces)
    their_d = group.swap(by_d, 1)
    by_y, by_d, near = lax.optimization_barrier((far_y, *run(keep_kernel, group, [square], by_d), near))
    their_y = group.swap(by_y, 1)
    if bits > 5:
        second = jnp.logical_not(group.bit(0))
        one, two = jnp.where(second, by_y, their_y), jnp.where(second, by_d, their_d)
        far = dot(*ordered(group.bit(1), jnp.where(second, their_y, by_y), jnp.where(second, their_d, by_d)))
        near = jnp.where(second, near, dot(*ordered(group.bit(1), wide, near)))
        three = dot(*ordered(group.bit(2), near, far))
        four = jnp.where(second, four, group.swap(four, 1))
        eight = dot(*ordered(group.bit(3), four, one))
        others = dot(*ordered(group.bit(3), two, three))
        wp, after = join(group, 3, one, wp, after)
        wp, after = join(group, 4, others, wp, after)
        total = dot(*ordered(group.bit(4), eight, others))
        return pairwise(group, range(5, bits), total, wp, after)[None, None]
    a, b = run(
        sides_kernel, group, [square] * 2, after, wp, near, wide, by_d, by_y, scratch=[square] * 3, weight=4
    )
    a, b = run(closer_kernel, group, [square] * 2, a, b, their_d)
    (result,) = run(result_kernel, group, [square], a, b, their_y, scratch=[square], weight=2)
    return result[None, None]


def solution(mesh):
    spec = P("outer", "inner", None, None)
    n_in, n_out = mesh.shape["inner"], mesh.shape["outer"]

    def gradient(slices, weight):
        return body(n_in, n_out, slices, weight)

    return jax.shard_map(gradient, mesh=mesh, in_specs=(spec, spec), out_specs=spec, check_vma=False)
```
